32 devices in a mesh: blk: 8 (over z, y), tok: 4 (over x, core).
Axes of the slice: x: 2, y: 2, z: 4, core: 2. Of those that a mesh axis runs over, the one named last changes fastest.
Arguments:
- queries: bfloat16 [256, 32, 128], P('blk'), may hold values from -0.5 to 0.5
- candidates: int32 [256, 4], P('blk'), may hold values from 0 to 7, all different within a row; in each aligned block of 32 rows (0 to 31, 32 to 63, ...) at most 32 rows name the same one
- passages: bfloat16 [8, 180, 32, 128], P('blk', 'tok'), may hold values from -0.5 to 0.5
- lengths: int32 [8, 32], P('blk'), may hold values from 1 to 180
Outputs:
- maxsim: float32 [256, 4, 32], P('blk', None, 'tok')
The draws below stay inside these ranges and needn't reach their ends.
Inputs may be any that keep to these rules, and one draw needn't show every extreme that they name: `candidates`: each row names 4 different blocks. Among the rows of one index of blk no block is named more than 32 times, and in every draw some block is named exactly 32 times by the rows of some index.
All inputs are finite; a program needn't handle non-finite values.
Results may differ from the reference program's by a relative error of at most 0.0003.
Values may be sent and summed in bfloat16 or wider, within the bound.
A program may use at most 64 MiB of HBM per device.

```python
import math
import jax
import jax.numpy as jnp
import numpy as np
from jax import lax

DIM = 128
QT = 32
PT = 180
PASS = 32
QDEV = 32
K = 4
BLOCKS = 8
QUERIES = 256
CAP = 32


def with_ends(drawn, rng, smallest, top_value):
    extent = drawn.shape
    spot = [jax.random.randint(jax.random.fold_in(rng, axis), (), 0, extent[axis]) for axis in range(len(extent))]
    drawn = drawn.at[tuple(spot)].set(smallest)
    longest = extent.index(max(extent))
    spot[longest] = (spot[longest] + 1) % extent[longest]
    return drawn.at[tuple(spot)].set(top_value)


def block_scale(stream_key, extent, split, low, top_value):
    def one(axis_at, parts):
        draws = jax.random.uniform(jax.random.fold_in(jax.random.fold_in(stream_key, 6), axis_at), (parts,), jnp.float32, low / len(split), top_value / len(split))
        return jnp.repeat(jnp.exp(draws), extent[axis_at] // parts).reshape((-1,) + (1,) * (len(extent) - axis_at - 1))

    loudness = one(*split[0])
    for cut in split[1:]:
        loudness = loudness * one(*cut)
    return loudness


def deal_out(key, own, number, rows, count, top, limit, slope):
    ranking = jax.random.permutation(key, count)
    crowded, ordinary = load_shares(count, rows * top, limit, slope, True), load_shares(count, rows * top, limit, slope, False)
    places = jnp.arange(count)

    def named(sizes, turn):
        used = int((sizes > 0).sum())
        fixed = max(1, used // 4)
        shifted = fixed + (places - fixed + turn * (used - fixed)) % max(1, count - fixed)
        return jnp.zeros((count,), jnp.int32).at[ranking[jnp.where(places < fixed, places, shifted)]].set(jnp.asarray(sizes, jnp.int32))

    sizes = jnp.where(number % 4 == 0, named(crowded, number // 4), named(ordinary, number - number // 4 - 1))
    mixed = jax.random.permutation(jax.random.fold_in(own, 3), count)
    source_of, receiver = mixed[0:count // 2 * 2:2], mixed[1:count // 2 * 2:2]
    room = jnp.minimum(sizes[source_of] - 1, limit - sizes[receiver]) // 2
    room = jnp.where((source_of == ranking[0]) | (receiver == ranking[0]) | (sizes[receiver] == 0), 0, jnp.maximum(room, 0))
    shifted = jax.random.randint(jax.random.fold_in(own, 4), (count // 2,), 0, 1 << 20) % (room + 1)
    sizes = sizes.at[source_of].add(-shifted).at[receiver].add(shifted)
    members = jnp.searchsorted(jnp.cumsum(sizes), jnp.arange(rows * top), side="right").astype(jnp.int32)
    listing = members.reshape(top, rows).T
    listing = listing[jax.random.permutation(jax.random.fold_in(own, 1), rows)]
    turn = jax.random.randint(jax.random.fold_in(own, 2), (rows, 1), 0, top)
    return jnp.take_along_axis(listing, (jnp.arange(top)[None, :] + turn) % top, axis=1)


def load_shares(count, total, reach, lean, full):
    weights = [(1 << 20) // math.isqrt(rank ** lean) + 1 for rank in range(1, count + 1)]
    largest = reach if full else min(reach, max(-(-total // count), total * weights[0] // sum(weights)))
    least = 1 if total - largest >= count - 1 else 0
    given, spare = [largest] + [least] * (count - 1), total - largest - least * (count - 1)
    while spare > 0:
        movable = [i for i in range(1, count) if given[i] < largest] or [i for i in range(1, count) if given[i] < reach]
        mass, remaining = sum([weights[i] for i in movable]), spare
        for i in movable:
            extra = min(reach - given[i], max(1, remaining * weights[i] // mass), spare)
            given[i] = given[i] + extra
            spare = spare - extra
    return np.array(given)


def bell_draw(key, dims, width, bound, cuts=(), kind=jnp.bfloat16):
    result = jax.random.normal(key, dims, jnp.float32) * width
    if len(cuts) > 0:
        result = block_scale(key, dims, cuts, -0.22, 0.18) * result
    return jnp.clip(result, min=-bound, max=bound).astype(kind)


def setup_inputs(seed: int = 0) -> dict:
    arg_keys = jax.random.split(jax.random.key(seed), 5)
    queries = bell_draw(arg_keys[0], (QUERIES, QT, DIM), DIM ** -0.5, 0.5, ((0, 8),))
    candidates_keys = jax.random.split(jax.random.fold_in(arg_keys[1], 1), QUERIES // QDEV)
    candidates_turns = jax.random.permutation(jax.random.fold_in(arg_keys[1], 3), QUERIES // QDEV)
    candidates = jax.vmap(lambda own, number: deal_out(jax.random.fold_in(arg_keys[1], 2), own, number, QDEV, BLOCKS, K, CAP, 2))(candidates_keys, candidates_turns).reshape((QUERIES, K))
    passages = bell_draw(arg_keys[2], (BLOCKS, PT, PASS, DIM), DIM ** -0.5, 0.5, ((0, 8), (1, 4)))
    lengths = with_ends(jax.random.randint(arg_keys[3], (BLOCKS, PASS), 1, PT + 1), jax.random.fold_in(arg_keys[3], 1), 1, PT).astype(jnp.int32)
    return dict(queries=queries, candidates=candidates, passages=passages, lengths=lengths)


NEGATIVE_FILL = -1.0e30


def reference(queries, candidates, passages, lengths):
    token_pos = jnp.arange(passages.shape[1], dtype=jnp.int32)

    def one_query(packed):
        query_tile, cand_row = packed
        query_wide = query_tile.astype(jnp.float32)

        def one_block(block_id):
            passage = passages[block_id].astype(jnp.float32)
            valid_mask = token_pos[:, None] < lengths[block_id][None, :]
            scores = jnp.einsum("qd,tpd->qtp", query_wide, passage)
            scores = jnp.where(valid_mask[None], scores, NEGATIVE_FILL)
            return jnp.sum(jnp.max(scores, axis=1), axis=0)

        return jax.vmap(one_block)(cand_row)

    return lax.map(one_query, (queries, candidates))
```

```python
import functools
import math

import jax
import jax.numpy as jnp
from jax import lax
from jax.experimental import pallas as pl
from jax.experimental.pallas import tpu as pltpu
from jax.sharding import PartitionSpec as P

NEGATIVE_FILL = -1e30


def block_maxima(query_rows, passage, valid_mask, piece_len):
    local_len = passage.shape[0]
    pass_width = passage.shape[1]
    pieces = local_len // piece_len

    def one_piece(step_idx, running):
        offset = step_idx * piece_len
        segment = lax.dynamic_slice_in_dim(passage, offset, piece_len, 0)
        kept_mask = lax.dynamic_slice_in_dim(valid_mask, offset, piece_len, 0)
        flattened = segment.reshape(piece_len * pass_width, segment.shape[2])
        scores = lax.dot_general(
            query_rows, flattened, (((1,), (1,)), ((), ())), preferred_element_type=jnp.float32
        )
        scores = scores.reshape(query_rows.shape[0], piece_len, pass_width)
        scores = jnp.where(kept_mask[None], scores, NEGATIVE_FILL)
        return jnp.maximum(running, jnp.max(scores, axis=1))

    start_max = jnp.full((query_rows.shape[0], pass_width), NEGATIVE_FILL, jnp.float32)
    return lax.fori_loop(0, pieces, one_piece, start_max)


def dispatch_shards(queries, candidates, passages, lengths):
    num_owners = lax.axis_size("blk")
    num_parts = lax.axis_size("tok")
    part_idx = lax.axis_index("tok")
    query_count, query_len, dim_width = queries.shape
    cand_count = candidates.shape[1]
    pass_width = passages.shape[2]
    part_width = pass_width // num_parts
    capacity = 2 * query_count * cand_count // num_owners
    pair_count = query_count * cand_count
    owner_ids = candidates.reshape(pair_count)
    pair_ids = jnp.arange(pair_count, dtype=jnp.int32)
    same = (owner_ids[:, None] == owner_ids[None, :]) & (pair_ids[None, :] < pair_ids[:, None])
    position = jnp.sum(same.astype(jnp.int32), axis=1)
    slot_ids = owner_ids * capacity + position
    dispatch = (
        jnp.arange(num_owners * capacity, dtype=jnp.int32)[:, None] == slot_ids[None, :]
    ).astype(jnp.bfloat16)
    repeated = jnp.repeat(queries.reshape(query_count, query_len * dim_width), cand_count, axis=0)
    outgoing = jnp.dot(dispatch, repeated, preferred_element_type=jnp.float32).astype(jnp.bfloat16)
    outgoing = outgoing.reshape(num_owners, capacity, query_len, dim_width)
    moved = lax.all_to_all(passages, "tok", split_axis=2, concat_axis=1, tiled=True)
    passage = moved[0]
    own_lengths = lax.dynamic_slice_in_dim(lengths[0], part_idx * part_width, part_width, 0)
    token_pos = jnp.arange(passage.shape[0], dtype=jnp.int32)
    valid_mask = token_pos[:, None] < own_lengths[None, :]
    score_len = passage.shape[0]
    score_width = passage.shape[1]
    piece_len = max((divisor for divisor in range(1, 17) if score_len % divisor == 0))
    received = lax.all_to_all(outgoing, "blk", split_axis=0, concat_axis=0, tiled=True)
    senders = received.shape[0]
    item_count = received.shape[1]
    slot_total = senders * item_count
    group_size = math.gcd(slot_total, 16)
    grouped = received.reshape(slot_total // group_size, group_size * query_len, dim_width)

    def per_group(query_rows):
        return block_maxima(query_rows, passage, valid_mask, piece_len)

    maxima = lax.map(per_group, grouped).reshape(senders, item_count, query_len, score_width)
    totals = jnp.sum(maxima, axis=2)
    returned = lax.all_to_all(totals, "blk", split_axis=0, concat_axis=0, tiled=True)
    flat_scores = returned.reshape(num_owners * capacity, part_width)
    picked = jnp.take(flat_scores, slot_ids, axis=0)
    return picked.reshape(query_count, cand_count, part_width)


LANES = 128
SUB = 8
MESH = pl.DeviceIdType.MESH


def dense_kernel(
    owners, parts, width, q_len, chunks,
    p_ref, q_ref, len_ref, cand_ref, out_ref,
    p_all, p_fix, p_first, q_all, acc, r_out, r_in,
    q_send, q_recv, near_send, near_recv, far_send, far_recv, hop_send, hop_recv,
    first_send, first_recv, r_send, r_recv,
):
    slots = p_ref.shape[0]
    piece = slots // chunks
    cols = q_len and q_all.shape[1]
    tiles = cols // LANES
    cand_count = cand_ref.shape[0]
    depth = owners // 2
    me, part = lax.axis_index("blk"), lax.axis_index("tok")
    z, y = me // 2, me % 2
    across, core = part // 2, part % 2
    partner = across * 2 + 1 - core
    opposite = (1 - across) * 2 + core
    diagonal = (1 - across) * 2 + 1 - core

    def remote(src, dst, send, recv, blk, tok):
        return pltpu.make_async_remote_copy(
            src_ref=src, dst_ref=dst, send_sem=send, recv_sem=recv,
            device_id={"blk": blk, "tok": tok}, device_id_type=MESH,
        )

    own_q = pltpu.make_async_copy(q_ref.at[part], q_all.at[me], q_recv.at[me])
    own_p = pltpu.make_async_copy(p_ref, p_all.at[0], near_recv.at[0])
    own_q.start()
    own_p.start()

    barrier = pltpu.get_barrier_semaphore()
    total = owners * parts
    flat = me * parts + part

    def greet(i, carry):
        other = (flat + i) % total
        pl.semaphore_signal(
            barrier, inc=1, device_id={"blk": other // parts, "tok": other % parts},
            device_id_type=MESH,
        )
        return carry

    lax.fori_loop(1, total, greet, 0)
    pl.semaphore_wait(barrier, total - 1)

    def q_copy(src, slot, way, blk):
        return remote(src, q_all.at[slot], q_send.at[slot, way], q_recv.at[slot], blk, part)

    def first_copy(j):
        return remote(
            p_ref.at[0], p_first, first_send.at[j], first_recv, me, (part + j) % parts
        )

    first_own = pltpu.make_async_copy(p_ref.at[0], p_first, first_recv)

    def far_copy(i):
        rows = pl.ds(i * piece, piece)
        return remote(
            p_ref.at[rows], p_all.at[2, rows], far_send.at[i], far_recv.at[i], me, opposite
        )

    def hop_copy(i):
        rows = pl.ds(i * piece, piece)
        return remote(
            p_all.at[2, rows], p_all.at[3, rows], hop_send.at[i], hop_recv.at[i], me, partner
        )

    near = remote(p_ref, p_all.at[1], near_send, near_recv.at[1], me, partner)

    def beside(slot, src):
        return q_copy(src, slot, 0, z * 2 + 1 - y)

    def along(slot, src, to_z):
        return q_copy(src, slot, 1, to_z * 2 + y)

    def along_down(slot, src):
        return q_copy(src, slot, 2, (z - 1) * 2 + y)

    @pl.when(part == 0)
    def _():
        first_own.start()
        for j in range(1, parts):
            first_copy(j).start()

    beside(me, q_ref.at[part]).start()

    @pl.when(z + 1 < depth)
    def _():
        along(me, q_ref.at[part], z + 1).start()

    @pl.when(z > 0)
    def _():
        along_down(me, q_ref.at[part]).start()

    near.start()
    for i in range(chunks):
        far_copy(i).start()

    def source(k):
        both = jnp.minimum(z, depth - 1 - z)
        paired = k <= 2 * both
        sign = jnp.where(
            paired, jnp.where(k % 2 == 1, -1, 1), jnp.where(z <= depth - 1 - z, 1, -1)
        )
        far = jnp.where(paired, (k + 1) // 2, k - both)
        return z + sign * far

    last = owners - 1

    def is_column(n):
        return (n == 0) | ((n % 2 == 1) & (n < last))

    def slot_of(n):
        k = jnp.where(n == last, depth - 1, jnp.where(n % 2 == 1, (n + 1) // 2, n // 2 - 1))
        k = jnp.where(n == 0, 0, k)
        return source(k) * 2 + jnp.where(is_column(n), y, 1 - y)

    def fix(place, tok):
        pos = lax.broadcasted_iota(jnp.int32, (slots, width, LANES), 0) + tok * slots
        kept = pos < len_ref[...][None]
        mine = p_all[place].astype(jnp.float32)
        first = p_first[...].astype(jnp.float32)
        p_fix[place] = jnp.where(kept, mine, first[None]).astype(p_fix.dtype)

    def best(slot, place):
        rows = p_fix[place].reshape(slots * width, LANES)
        scores = lax.dot_general(
            rows, q_all[slot], (((1,), (1,)), ((), ())), preferred_element_type=jnp.float32
        )
        return jnp.max(scores.reshape(slots, width, cols), axis=0)

    first_own.wait()
    own_p.wait()
    fix(0, part)
    near.wait_recv()
    fix(1, partner)

    def onward(n):
        slot = slot_of(n)
        from_z = slot // 2
        src = q_all.at[slot]
        up = (from_z < z) & (z + 1 < depth)
        down = (from_z > z) & (z > 0)
        return slot, src, up, down

    def early(n, carry):
        slot, src, up, down = onward(n)
        pltpu.make_async_copy(src, src, q_recv.at[slot]).wait()

        @pl.when(is_column(n) & (n > 0))
        def _():
            beside(slot, src).start()

            @pl.when(up)
            def _():
                along(slot, src, z + 1).start()

            @pl.when(down)
            def _():
                along_down(slot, src).start()

        for i in range(chunks):

            @pl.when(n == 2 * i + 2)
            def _():
                far_copy(i).wait_recv()
                hop_copy(i).start()

        acc[n] = jnp.maximum(best(slot, 0), best(slot, 1))
        return carry

    lax.fori_loop(0, owners, early, 0)

    for i in range(chunks):
        hop_copy(i).wait_recv()
    fix(2, opposite)
    fix(3, diagonal)

    lane = lax.broadcasted_iota(jnp.int32, (SUB, LANES), 1)

    def r_copy(slot, j):
        tok = (part + j) % parts
        return remote(
            r_out.at[slot], r_in.at[me, part], r_send.at[slot, tok], r_recv.at[me, part], slot, tok
        )

    def late(n, carry):
        slot = slot_of(n)
        found = jnp.maximum(acc[n], jnp.maximum(best(slot, 2), best(slot, 3)))
        tile = jnp.zeros((SUB, LANES), jnp.float32)
        for g in range(tiles):
            sums = found[:, g * LANES : (g + 1) * LANES]
            step = q_len // 2
            while step:
                sums = sums + pltpu.roll(sums, LANES - step, 1)
                step //= 2
            for group in range(parts):
                at = group * tiles + g
                piece_sums = sums[group * SUB : (group + 1) * SUB]
                if at:
                    piece_sums = pltpu.roll(piece_sums, at, 1)
                tile = jnp.where(lane % q_len == at, piece_sums, tile)
        r_out[slot] = tile
        for j in range(1, parts):
            r_copy(slot, j).start()

        @pl.when(n > 0)
        def _():
            r_copy(slot, 0).start()

        @pl.when(n == 0)
        def _():
            r_in[me, part] = tile

        return carry

    lax.fori_loop(0, owners, late, 0)

    def drain(n, carry):
        slot, src, up, down = onward(n)

        @pl.when(is_column(n))
        def _():
            beside(slot, src).wait_send()

            @pl.when(up | ((n == 0) & (z + 1 < depth)))
            def _():
                along(slot, src, z + 1).wait_send()

            @pl.when(down | ((n == 0) & (z > 0)))
            def _():
                along_down(slot, src).wait_send()

        for j in range(parts):

            @pl.when((n > 0) | (j > 0))
            def _():
                tok = (part + j) % parts
                r_copy(slot, j).wait_send()
                here = r_in.at[slot, tok]
                pltpu.make_async_copy(here, here, r_recv.at[slot, tok]).wait()

        return carry

    lax.fori_loop(0, owners, drain, 0)
    near.wait_send()
    for i in range(chunks):
        far_copy(i).wait_send()
        hop_copy(i).wait_send()

    @pl.when(part == 0)
    def _():
        for j in range(1, parts):
            first_copy(j).wait_send()

    picked = [jnp.zeros((SUB, LANES), jnp.float32) for _ in range(cand_count)]
    for blk in range(owners):
        merged = jnp.zeros((SUB, LANES), jnp.float32)
        for tok in range(parts):
            moved = pltpu.roll(r_in[blk, tok], (tiles * (tok - part) + LANES) % LANES, 1)
            merged = jnp.where((lane % q_len) // tiles == tok, moved, merged)
        for k in range(cand_count):
            picked[k] = jnp.where(cand_ref[k : k + 1, :] == blk, merged, picked[k])
    for k in range(cand_count):
        out_ref[k] = picked[k]


def dense_shards(queries, candidates, passages, lengths):
    owners, parts = lax.axis_size("blk"), lax.axis_size("tok")
    query_count, q_len, dim = queries.shape
    cand_count = candidates.shape[1]
    slots, width = passages.shape[1], passages.shape[2]
    share = query_count // parts
    cols = share * q_len
    tiles = cols // LANES
    per = LANES // q_len
    chunks = 3 if slots % 3 == 0 else 1
    used = parts * tiles
    cand = candidates.reshape(parts, tiles, per, cand_count).transpose(3, 2, 0, 1)
    cand = cand.reshape(cand_count, per, used)
    cand = jnp.pad(cand, ((0, 0), (0, 0), (0, q_len - used))).reshape(cand_count, LANES)
    limits = jnp.broadcast_to(lengths[0][:, None], (width, LANES))
    dma = pltpu.SemaphoreType.DMA
    out = pl.pallas_call(
        functools.partial(dense_kernel, owners, parts, width, q_len, chunks),
        out_shape=jax.ShapeDtypeStruct((cand_count, SUB, LANES), jnp.float32),
        in_specs=[pl.BlockSpec(memory_space=pl.ANY)] * 2
        + [pl.BlockSpec(memory_space=pltpu.VMEM)] * 2,
        out_specs=pl.BlockSpec(memory_space=pltpu.VMEM),
        scratch_shapes=[
            pltpu.VMEM((4, slots, width, dim), passages.dtype),
            pltpu.VMEM((4, slots, width, dim), passages.dtype),
            pltpu.VMEM((width, dim), passages.dtype),
            pltpu.VMEM((owners, cols, dim), queries.dtype),
            pltpu.VMEM((owners, width, cols), jnp.float32),
            pltpu.VMEM((owners, SUB, LANES), jnp.float32),
            pltpu.VMEM((owners, parts, SUB, LANES), jnp.float32),
            dma((owners, 3)),
            dma((owners,)),
            dma,
            dma((2,)),
            dma((chunks,)),
            dma((chunks,)),
            dma((chunks,)),
            dma((chunks,)),
            dma((parts,)),
            dma,
            dma((owners, parts)),
            dma((owners, parts)),
        ],
        compiler_params=pltpu.CompilerParams(
            collective_id=0, has_side_effects=True, vmem_limit_bytes=48 * 1024 * 1024
        ),
    )(passages[0], queries.reshape(parts, cols, dim), limits, cand)
    out = out.reshape(cand_count, SUB, per, q_len)[:, :, :, :used]
    out = out.reshape(cand_count, SUB, per, parts, tiles).transpose(3, 4, 2, 0, 1)
    return out.reshape(query_count, cand_count, SUB)


def dense_fits(mesh, queries, candidates, passages):
    owners, parts = mesh.shape["blk"], mesh.shape["tok"]
    query_count, q_len = queries.shape[0] // owners, queries.shape[1]
    if owners % 2 or parts != 4 or query_count % parts or LANES % q_len:
        return False
    cols = query_count // parts * q_len
    return (
        owners <= 4 * candidates.shape[1]
        and passages.shape[0] == owners
        and cols % LANES == 0
        and parts * (cols // LANES) <= q_len
        and passages.shape[2] == parts * SUB
        and passages.shape[3] == LANES
        and passages.shape[1] % parts == 0
    )


def solution(mesh):
    in_specs = (P("blk", None, None), P("blk", None), P("blk", "tok", None, None), P("blk", None))
    out_specs = P("blk", None, "tok")

    def run(queries, candidates, passages, lengths):
        fits = dense_fits(mesh, queries, candidates, passages)
        body = dense_shards if fits else dispatch_shards
        return jax.shard_map(
            body, mesh=mesh, in_specs=in_specs, out_specs=out_specs, check_vma=False
        )(queries, candidates, passages, lengths)

    return run
```

```python
import functools
import math

import jax
import jax.numpy as jnp
from jax import lax
from jax.experimental import pallas as pl
from jax.experimental.pallas import tpu as pltpu
from jax.sharding import PartitionSpec as P

NEGATIVE_FILL = -1e30


def block_maxima(query_rows, passage, valid_mask, piece_len):
    local_len = passage.shape[0]
    pass_width = passage.shape[1]
    pieces = local_len // piece_len

    def one_piece(step_idx, running):
        offset = step_idx * piece_len
        segment = lax.dynamic_slice_in_dim(passage, offset, piece_len, 0)
        kept_mask = lax.dynamic_slice_in_dim(valid_mask, offset, piece_len, 0)
        flattened = segment.reshape(piece_len * pass_width, segment.shape[2])
        scores = lax.dot_general(
            query_rows, flattened, (((1,), (1,)), ((), ())), preferred_element_type=jnp.float32
        )
        scores = scores.reshape(query_rows.shape[0], piece_len, pass_width)
        scores = jnp.where(kept_mask[None], scores, NEGATIVE_FILL)
        return jnp.maximum(running, jnp.max(scores, axis=1))

    start_max = jnp.full((query_rows.shape[0], pass_width), NEGATIVE_FILL, jnp.float32)
    return lax.fori_loop(0, pieces, one_piece, start_max)


def dispatch_shards(queries, candidates, passages, lengths):
    num_owners = lax.axis_size("blk")
    num_parts = lax.axis_size("tok")
    part_idx = lax.axis_index("tok")
    query_count, query_len, dim_width = queries.shape
    cand_count = candidates.shape[1]
    pass_width = passages.shape[2]
    part_width = pass_width // num_parts
    capacity = 2 * query_count * cand_count // num_owners
    pair_count = query_count * cand_count
    owner_ids = candidates.reshape(pair_count)
    pair_ids = jnp.arange(pair_count, dtype=jnp.int32)
    same = (owner_ids[:, None] == owner_ids[None, :]) & (pair_ids[None, :] < pair_ids[:, None])
    position = jnp.sum(same.astype(jnp.int32), axis=1)
    slot_ids = owner_ids * capacity + position
    dispatch = (
        jnp.arange(num_owners * capacity, dtype=jnp.int32)[:, None] == slot_ids[None, :]
    ).astype(jnp.bfloat16)
    repeated = jnp.repeat(queries.reshape(query_count, query_len * dim_width), cand_count, axis=0)
    outgoing = jnp.dot(dispatch, repeated, preferred_element_type=jnp.float32).astype(jnp.bfloat16)
    outgoing = outgoing.reshape(num_owners, capacity, query_len, dim_width)
    moved = lax.all_to_all(passages, "tok", split_axis=2, concat_axis=1, tiled=True)
    passage = moved[0]
    own_lengths = lax.dynamic_slice_in_dim(lengths[0], part_idx * part_width, part_width, 0)
    token_pos = jnp.arange(passage.shape[0], dtype=jnp.int32)
    valid_mask = token_pos[:, None] < own_lengths[None, :]
    score_len = passage.shape[0]
    score_width = passage.shape[1]
    piece_len = max((divisor for divisor in range(1, 17) if score_len % divisor == 0))
    received = lax.all_to_all(outgoing, "blk", split_axis=0, concat_axis=0, tiled=True)
    senders = received.shape[0]
    item_count = received.shape[1]
    slot_total = senders * item_count
    group_size = math.gcd(slot_total, 16)
    grouped = received.reshape(slot_total // group_size, group_size * query_len, dim_width)

    def per_group(query_rows):
        return block_maxima(query_rows, passage, valid_mask, piece_len)

    maxima = lax.map(per_group, grouped).reshape(senders, item_count, query_len, score_width)
    totals = jnp.sum(maxima, axis=2)
    returned = lax.all_to_all(totals, "blk", split_axis=0, concat_axis=0, tiled=True)
    flat_scores = returned.reshape(num_owners * capacity, part_width)
    picked = jnp.take(flat_scores, slot_ids, axis=0)
    return picked.reshape(query_count, cand_count, part_width)


LANES = 128
SUB = 8
MESH = pl.DeviceIdType.MESH


def dense_kernel(
    owners, parts, width, q_len, chunks,
    p_ref, q_ref, len_ref, cand_ref, out_ref,
    p_all, p_fix, p_first, q_all, acc, r_out, r_in,
    q_send, q_recv, near_send, near_recv, far_send, far_recv, hop_send, hop_recv,
    first_send, first_recv, r_send, r_recv,
):
    slots = p_ref.shape[0]
    piece = slots // chunks
    cols = q_all.shape[1]
    tiles = cols // LANES
    per = LANES // q_len
    cand_count = cand_ref.shape[0]
    depth = owners // 2
    me, part = lax.axis_index("blk"), lax.axis_index("tok")
    z, y = me // 2, me % 2
    across, core = part // 2, part % 2
    partner = across * 2 + 1 - core
    opposite = (1 - across) * 2 + core
    diagonal = (1 - across) * 2 + 1 - core

    def remote(src, dst, send, recv, blk, tok):
        return pltpu.make_async_remote_copy(
            src_ref=src, dst_ref=dst, send_sem=send, recv_sem=recv,
            device_id={"blk": blk, "tok": tok}, device_id_type=MESH,
        )

    own_q = pltpu.make_async_copy(q_ref.at[part], q_all.at[me], q_recv.at[me])
    own_p = pltpu.make_async_copy(p_ref, p_all.at[0], near_recv.at[0])
    own_q.start()
    own_p.start()

    barrier = pltpu.get_barrier_semaphore()

    def greet(blk, tok):
        pl.semaphore_signal(
            barrier, inc=1, device_id={"blk": blk, "tok": tok}, device_id_type=MESH
        )

    def in_column(j):
        return (z + j) % depth * 2 + y

    for j in range(1, depth):
        greet(in_column(j), part)
    greet(z * 2 + 1 - y, part)
    for j in range(1, parts):
        greet(me, (part + j) % parts)

    def query_of(at):
        rest = at % q_len
        query = rest // tiles * (tiles * per) + rest % tiles * per + at // q_len
        return jnp.where(rest < parts * tiles, query, -1)

    queries = cand_ref.shape[1]
    place = lax.broadcasted_iota(jnp.int32, (queries, LANES), 0)
    spread = place == query_of(lax.broadcasted_iota(jnp.int32, (queries, LANES), 1))
    cand = jnp.dot(
        cand_ref[...].astype(jnp.float32).astype(jnp.bfloat16),
        spread.astype(jnp.float32).astype(jnp.bfloat16),
        preferred_element_type=jnp.float32,
    )
    place = lax.broadcasted_iota(jnp.int32, (width, width), 0)
    same = place == lax.broadcasted_iota(jnp.int32, (width, width), 1)
    counts = jnp.broadcast_to(len_ref[...].astype(jnp.float32), (width, width))
    limit = jnp.sum(jnp.where(same, counts, 0.0), axis=1, keepdims=True)
    limit = jnp.broadcast_to(limit, (width, LANES))

    pl.semaphore_wait(barrier, depth - 1 + 1 + parts - 1)

    def q_copy(src, slot, way, blk):
        return remote(src, q_all.at[slot], q_send.at[slot, way], q_recv.at[slot], blk, part)

    def first_copy(j):
        return remote(
            p_ref.at[0], p_first, first_send.at[j], first_recv, me, (part + j) % parts
        )

    first_own = pltpu.make_async_copy(p_ref.at[0], p_first, first_recv)

    def far_copy(i):
        rows = pl.ds(i * piece, piece)
        return remote(
            p_ref.at[rows], p_all.at[2, rows], far_send.at[i], far_recv.at[i], me, opposite
        )

    def hop_copy(i):
        rows = pl.ds(i * piece, piece)
        return remote(
            p_all.at[2, rows], p_all.at[3, rows], hop_send.at[i], hop_recv.at[i], me, partner
        )

    near = remote(p_ref, p_all.at[1], near_send, near_recv.at[1], me, partner)

    def beside(slot, src):
        return q_copy(src, slot, 0, z * 2 + 1 - y)

    def along(j):
        return q_copy(q_ref.at[part], me, j, in_column(j))

    @pl.when(part == 0)
    def _():
        first_own.start()
        for j in range(1, parts):
            first_copy(j).start()

    beside(me, q_ref.at[part]).start()
    for j in range(1, depth):
        along(j).start()

    near.start()
    for i in range(chunks):
        far_copy(i).start()

    def source(k):
        both = jnp.minimum(z, depth - 1 - z)
        paired = k <= 2 * both
        sign = jnp.where(
            paired, jnp.where(k % 2 == 1, -1, 1), jnp.where(z <= depth - 1 - z, 1, -1)
        )
        far = jnp.where(paired, (k + 1) // 2, k - both)
        return z + sign * far

    last = owners - 1

    def is_column(n):
        return (n == 0) | ((n % 2 == 1) & (n < last))

    def slot_of(n):
        k = jnp.where(n == last, depth - 1, jnp.where(n % 2 == 1, (n + 1) // 2, n // 2 - 1))
        k = jnp.where(n == 0, 0, k)
        return source(k) * 2 + jnp.where(is_column(n), y, 1 - y)

    def fix(place, tok):
        pos = lax.broadcasted_iota(jnp.int32, (slots, width, LANES), 0) + tok * slots
        kept = pos.astype(jnp.float32) < limit[None]
        mine = p_all[place].astype(jnp.float32)
        first = p_first[...].astype(jnp.float32)
        p_fix[place] = jnp.where(kept, mine, first[None]).astype(p_fix.dtype)

    def best(slot, place):
        rows = p_fix[place].reshape(slots * width, LANES)
        scores = lax.dot_general(
            rows, q_all[slot], (((1,), (1,)), ((), ())), preferred_element_type=jnp.float32
        )
        return jnp.max(scores.reshape(slots, width, cols), axis=0)

    first_own.wait()
    own_p.wait()
    fix(0, part)
    near.wait_recv()
    fix(1, partner)

    def arrive(n):
        slot = slot_of(n)
        src = q_all.at[slot]
        pltpu.make_async_copy(src, src, q_recv.at[slot]).wait()

        @pl.when(is_column(n) & (n > 0))
        def _():
            beside(slot, src).start()

        return slot

    half = owners // 2

    def early(n, carry):
        slot = arrive(n)
        for i in range(chunks):

            @pl.when(n == min(i + 1, half - 1))
            def _():
                far_copy(i).wait_recv()
                hop_copy(i).start()

        acc[n] = jnp.maximum(best(slot, 0), best(slot, 1))
        return carry

    lane = lax.broadcasted_iota(jnp.int32, (SUB, LANES), 1)

    def r_copy(slot, j):
        tok = (part + j) % parts
        return remote(
            r_out.at[slot], r_in.at[me, part], r_send.at[slot, tok], r_recv.at[me, part], slot, tok
        )

    def late(n):
        slot = slot_of(n)
        found = jnp.maximum(acc[n], jnp.maximum(best(slot, 2), best(slot, 3)))
        tile = jnp.zeros((SUB, LANES), jnp.float32)
        for g in range(tiles):
            sums = found[:, g * LANES : (g + 1) * LANES]
            step = q_len // 2
            while step:
                sums = sums + pltpu.roll(sums, LANES - step, 1)
                step //= 2
            for group in range(parts):
                at = group * tiles + g
                piece_sums = sums[group * SUB : (group + 1) * SUB]
                if at:
                    piece_sums = pltpu.roll(piece_sums, at, 1)
                tile = jnp.where(lane % q_len == at, piece_sums, tile)
        r_out[slot] = tile
        for j in range(1, parts):
            r_copy(slot, j).start()

        @pl.when(n > 0)
        def _():
            r_copy(slot, 0).start()

        @pl.when(n == 0)
        def _():
            r_in[me, part] = tile

    lax.fori_loop(0, half, early, 0)
    for i in range(chunks):
        hop_copy(i).wait_recv()
    fix(2, opposite)
    fix(3, diagonal)

    def both(i, carry):
        n = lax.select(i % 2 == 1, half + i // 2, i // 2)

        @pl.when(i % 2 == 1)
        def _():
            slot = arrive(n)
            acc[n] = jnp.maximum(best(slot, 0), best(slot, 1))

        late(n)
        return carry

    lax.fori_loop(0, owners, both, 0)

    for j in range(1, depth):
        along(j).wait_send()

    def drain(n, carry):
        slot = slot_of(n)

        @pl.when(is_column(n))
        def _():
            beside(slot, q_all.at[slot]).wait_send()

        for j in range(parts):

            @pl.when((n > 0) | (j > 0))
            def _():
                tok = (part + j) % parts
                r_copy(slot, j).wait_send()
                here = r_in.at[slot, tok]
                pltpu.make_async_copy(here, here, r_recv.at[slot, tok]).wait()

        return carry

    lax.fori_loop(0, owners, drain, 0)
    near.wait_send()
    for i in range(chunks):
        far_copy(i).wait_send()
        hop_copy(i).wait_send()

    @pl.when(part == 0)
    def _():
        for j in range(1, parts):
            first_copy(j).wait_send()

    picked = [jnp.zeros((SUB, LANES), jnp.float32) for _ in range(cand_count)]
    for blk in range(owners):
        merged = jnp.zeros((SUB, LANES), jnp.float32)
        for tok in range(parts):
            moved = pltpu.roll(r_in[blk, tok], (tiles * (tok - part) + LANES) % LANES, 1)
            merged = jnp.where((lane % q_len) // tiles == tok, moved, merged)
        for k in range(cand_count):
            picked[k] = jnp.where(cand[k : k + 1, :] == blk, merged, picked[k])
    at = lax.broadcasted_iota(jnp.int32, (LANES, queries), 0)
    gather = query_of(at) == lax.broadcasted_iota(jnp.int32, (LANES, queries), 1)
    rows = jnp.dot(
        jnp.concatenate(picked, axis=0), gather.astype(jnp.float32),
        precision=lax.Precision.HIGHEST, preferred_element_type=jnp.float32,
    )
    for k in range(cand_count):
        out_ref[k] = rows[k * SUB : (k + 1) * SUB]


def dense_shards(queries, candidates, passages, lengths):
    owners, parts = lax.axis_size("blk"), lax.axis_size("tok")
    query_count, q_len, dim = queries.shape
    cand_count = candidates.shape[1]
    slots, width = passages.shape[1], passages.shape[2]
    share = query_count // parts
    cols = share * q_len
    chunks = 3 if slots % 3 == 0 else 1
    dma = pltpu.SemaphoreType.DMA
    out = pl.pallas_call(
        functools.partial(dense_kernel, owners, parts, width, q_len, chunks),
        out_shape=jax.ShapeDtypeStruct((cand_count, SUB, query_count), jnp.float32),
        in_specs=[pl.BlockSpec(memory_space=pl.ANY)] * 2
        + [pl.BlockSpec(memory_space=pltpu.VMEM)] * 2,
        out_specs=pl.BlockSpec(memory_space=pltpu.VMEM),
        scratch_shapes=[
            pltpu.VMEM((4, slots, width, dim), passages.dtype),
            pltpu.VMEM((4, slots, width, dim), passages.dtype),
            pltpu.VMEM((width, dim), passages.dtype),
            pltpu.VMEM((owners, cols, dim), queries.dtype),
            pltpu.VMEM((owners, width, cols), jnp.float32),
            pltpu.VMEM((owners, SUB, LANES), jnp.float32),
            pltpu.VMEM((owners, parts, SUB, LANES), jnp.float32),
            dma((owners, owners // 2)),
            dma((owners,)),
            dma,
            dma((2,)),
            dma((chunks,)),
            dma((chunks,)),
            dma((chunks,)),
            dma((chunks,)),
            dma((parts,)),
            dma,
            dma((owners, parts)),
            dma((owners, parts)),
        ],
        compiler_params=pltpu.CompilerParams(
            collective_id=0, has_side_effects=True, vmem_limit_bytes=60 * 1024 * 1024
        ),
    )(passages[0], queries.reshape(parts, cols, dim), lengths, candidates.T)
    return out.transpose(2, 0, 1)


def dense_fits(mesh, queries, candidates, passages):
    owners, parts = mesh.shape["blk"], mesh.shape["tok"]
    query_count, q_len = queries.shape[0] // owners, queries.shape[1]
    if owners % 2 or parts != 4 or query_count % parts or LANES % q_len:
        return False
    cols = query_count // parts * q_len
    return (
        owners <= 4 * candidates.shape[1]
        and passages.shape[0] == owners
        and cols % LANES == 0
        and parts * (cols // LANES) <= q_len
        and passages.shape[2] == parts * SUB
        and passages.shape[3] == LANES
        and passages.shape[1] % parts == 0
    )


def solution(mesh):
    in_specs = (P("blk", None, None), P("blk", None), P("blk", "tok", None, None), P("blk", None))
    out_specs = P("blk", None, "tok")

    def run(queries, candidates, passages, lengths):
        fits = dense_fits(mesh, queries, candidates, passages)
        body = dense_shards if fits else dispatch_shards
        return jax.shard_map(
            body, mesh=mesh, in_specs=in_specs, out_specs=out_specs, check_vma=False
        )(queries, candidates, passages, lengths)

    return run
```
